512 devices in a mesh: parts: 512 (over x, y, z, core).
Axes of the slice: x: 4, y: 4, z: 16, core: 2. Of those that a mesh axis runs over, the one named last changes fastest.
Arguments:
- modal_state: float32 [9, 35, 65536], P(None, None, 'parts'), may hold values from -6 to 6
- density: float32 [65536], P('parts'), may hold values from 1 to 3
- shear_modulus: float32 [65536], P('parts'), may hold values from 0.3 to 1
- lame_lambda: float32 [65536], P('parts'), may hold values from 0.3 to 1.5
- geometry: float32 [3, 3, 65536], P(None, None, 'parts'), may hold values from -3 to 3
- normals: float32 [4, 3, 65536], P(None, None, 'parts'), may hold values from -3 to 3
- stiffness: float32 [3, 35, 35], replicated, may hold values from -0.625 to 0.625
- face_projection: float32 [4, 21, 35], replicated, may hold values from -1 to 1
- lift_matrices: float32 [4, 35, 21], replicated, may hold values from -1.25 to 1.25
- cluster: int32 [65536], P('parts'), may hold values from 0 to 1, as said below
- neighbour: int32 [4, 65536], P(None, 'parts'), may hold values from 0 to 641, as said below
- send_list: int32 [4, 16384], P(None, 'parts'), may hold values from 0 to 511, as said below
- fault_plus: int32 [65536], P('parts'), may hold values from 0 to 511, as said below
- fault_minus: int32 [65536], P('parts'), may hold values from 0 to 511, as said below
- direct_effect: float32 [21, 65536], P(None, 'parts'), may hold values from 0.1 to 0.3
- fault_state: float32 [21, 65536], P(None, 'parts'), may hold values from 0.3 to 0.6
- slip_rate: float32 [21, 65536], P(None, 'parts'), may hold values from 0.05 to 1
- shear_stress: float32 [2, 21, 65536], P(None, None, 'parts'), may hold values from -4 to 4
- normal_stress: float32 [21, 65536], P(None, 'parts'), may hold values from -3 to -1
Outputs:
- new_state: float32 [9, 35, 65536], P(None, None, 'parts')
- new_slip: float32 [21, 65536], P(None, 'parts')
- new_fault_state: float32 [21, 65536], P(None, 'parts')
The draws below stay inside these ranges and needn't reach their ends.
Inputs may be any that keep to these rules, and one draw needn't show every extreme that they name: 1 marks the slower cluster; every element with a fault side has 0. `neighbour`: on each device, values 4 * 128 + k for k < 128 appear exactly once each; 640 marks absorbing faces (32 of them a device) and 641 marks exactly the faces listed in fault_plus and fault_minus. `send_list`: local face indices f * 128 + e. `fault_plus`: distinct local face indices of one device, disjoint from fault_minus. `fault_minus`: distinct local face indices of one device; entry j is the minus side of entry j of fault_plus on the device 8 places lower, cyclically.
All inputs are finite; a program needn't handle non-finite values.
Results may differ from the reference program's by a relative error of at most 0.0003.
Values sent between devices are 32-bit elements; how exact they have to be, the bound alone decides.
A program may use at most 128 MiB of HBM per device.

```python
import math
from functools import partial
import jax
import jax.numpy as jnp
from jax import lax

BASIS = 35
FACE_BASIS = 21
QUANTITIES = 9
DERIVS = 4
ITERS = 10
STRIDE = 8
E_DEV = 128
SLOTS = 32
F_DEV = 128
ELEMS = 65536
FAULTS = 65536
N_PARTS = 512


def layout_one(device_key):
    faces_total = 4 * E_DEV
    remote = 4 * SLOTS
    subkeys = jax.random.split(device_key, 5)
    shuffled = jax.random.permutation(subkeys[0], faces_total).astype(jnp.int32)
    links_flat = jax.random.randint(subkeys[1], (faces_total,), 0, faces_total, dtype=jnp.int32)
    links_flat = links_flat.at[shuffled[:remote]].set(faces_total + jnp.arange(remote, dtype=jnp.int32))
    links_flat = links_flat.at[shuffled[remote:remote + 2 * F_DEV]].set(faces_total + remote + 1)
    links_flat = links_flat.at[shuffled[remote + 2 * F_DEV:remote + 2 * F_DEV + SLOTS]].set(faces_total + remote)
    plus_sides = shuffled[remote:remote + F_DEV]
    minus_sides = shuffled[remote + F_DEV:remote + 2 * F_DEV]
    slow_share = jax.random.randint(subkeys[2], (), 20, 81, dtype=jnp.int32)
    dice_rolls = jax.random.randint(subkeys[3], (E_DEV,), 0, 100, dtype=jnp.int32)
    cluster_ids = (dice_rolls < slow_share).astype(jnp.int32)
    cluster_ids = cluster_ids.at[shuffled[remote:remote + 2 * F_DEV] % E_DEV].set(0)
    outgoing = jax.random.randint(subkeys[4], (4, SLOTS), 0, faces_total, dtype=jnp.int32)
    return (cluster_ids, links_flat.reshape(4, E_DEV), outgoing, plus_sides, minus_sides)


def layout_all(key):
    base_key = jax.random.fold_in(key, 17)
    device_keys = jax.vmap(partial(jax.random.fold_in, base_key))(jnp.arange(N_PARTS))
    cluster_ids, links_all, outgoing, plus_sides, minus_sides = jax.vmap(layout_one)(device_keys)
    return (cluster_ids.reshape(-1), jnp.transpose(links_all, (1, 0, 2)).reshape(4, -1), jnp.transpose(outgoing, (1, 0, 2)).reshape(4, -1), plus_sides.reshape(-1), minus_sides.reshape(-1))


def draw_cluster(key, part):
    return layout_all(key)[0]


def draw_neighbour(key, part):
    return layout_all(key)[1]


def draw_send_list(key, part):
    return layout_all(key)[2]


def draw_fault_plus(key, part):
    return layout_all(key)[3]


def draw_fault_minus(key, part):
    return layout_all(key)[4]


def shard_levels(key, dims, cuts, low, largest):
    loudness = 1.0
    for axis_at, blocks in cuts:
        heights = jax.random.uniform(jax.random.fold_in(jax.random.fold_in(key, 6), axis_at), (blocks,), jnp.float32, low / len(cuts), largest / len(cuts))
        loudness = loudness * jnp.repeat(jnp.exp(heights), dims[axis_at] // blocks).reshape((-1,) + (1,) * (len(dims) - 1 - axis_at))
    return loudness


def gaussian(key, dims, scale, reach, cuts=(), held_as=jnp.bfloat16):
    result = scale * jax.random.normal(key, dims, jnp.float32)
    if cuts:
        result = result * shard_levels(key, dims, cuts, -0.22, 0.18)
    return jnp.clip(result, -reach, reach).astype(held_as)


def setup_inputs(seed: int = 0) -> dict:
    seeds = jax.random.split(jax.random.key(seed), 20)
    return {
        "modal_state": gaussian(seeds[0], (QUANTITIES, BASIS, ELEMS), 1.0, 6.0, ((2, 512),), jnp.float32),
        "density": jnp.clip(jnp.exp(math.log(3.0) - 1.0986123 * jax.random.uniform(seeds[1], (ELEMS,), jnp.float32) ** shard_levels(seeds[1], (ELEMS,), ((0, 512),), -0.2, 0.2)), 1.0, 3.0),
        "shear_modulus": jnp.clip(jnp.exp(math.log(1.0) - 1.2039728 * jax.random.uniform(seeds[2], (ELEMS,), jnp.float32) ** shard_levels(seeds[2], (ELEMS,), ((0, 512),), -0.2, 0.2)), 0.3, 1.0),
        "lame_lambda": jnp.clip(jnp.exp(math.log(1.5) - 1.60943787 * jax.random.uniform(seeds[3], (ELEMS,), jnp.float32) ** shard_levels(seeds[3], (ELEMS,), ((0, 512),), -0.2, 0.2)), 0.3, 1.5),
        "geometry": gaussian(seeds[4], (3, 3, ELEMS), 0.5, 3.0, ((2, 512),), jnp.float32),
        "normals": gaussian(seeds[5], (4, 3, ELEMS), 0.5, 3.0, ((2, 512),), jnp.float32),
        "stiffness": gaussian(seeds[6], (3, BASIS, BASIS), (3 * BASIS) ** -0.5, 0.625, (), jnp.float32),
        "face_projection": gaussian(seeds[7], (4, FACE_BASIS, BASIS), BASIS ** -0.5, 1.0, (), jnp.float32),
        "lift_matrices": gaussian(seeds[8], (4, BASIS, FACE_BASIS), FACE_BASIS ** -0.5, 1.25, (), jnp.float32),
        "cluster": draw_cluster(jax.random.fold_in(seeds[19], 71), 0),
        "neighbour": draw_neighbour(jax.random.fold_in(seeds[19], 71), 0),
        "send_list": draw_send_list(jax.random.fold_in(seeds[19], 71), 0),
        "fault_plus": draw_fault_plus(jax.random.fold_in(seeds[19], 71), 0),
        "fault_minus": draw_fault_minus(jax.random.fold_in(seeds[19], 71), 0),
        "direct_effect": jnp.clip(jnp.exp(math.log(0.3) - 1.0986123 * jax.random.uniform(seeds[14], (FACE_BASIS, FAULTS), jnp.float32) ** shard_levels(seeds[14], (FACE_BASIS, FAULTS), ((1, 512),), -0.2, 0.2)), 0.1, 0.3),
        "fault_state": jnp.clip(0.3 + 0.3 * jax.random.uniform(seeds[15], (FACE_BASIS, FAULTS), jnp.float32) ** shard_levels(seeds[15], (FACE_BASIS, FAULTS), ((1, 512),), -0.2, 0.2), 0.3, 0.6),
        "slip_rate": jnp.clip(jnp.exp(math.log(1.0) - 2.9957323 * jax.random.uniform(seeds[16], (FACE_BASIS, FAULTS), jnp.float32) ** shard_levels(seeds[16], (FACE_BASIS, FAULTS), ((1, 512),), -0.2, 0.2)), 0.05, 1.0),
        "shear_stress": gaussian(seeds[17], (2, FACE_BASIS, FAULTS), 0.7, 4.0, ((2, 512),), jnp.float32),
        "normal_stress": jnp.clip(-3.0 + 2.0 * jax.random.uniform(seeds[18], (FACE_BASIS, FAULTS), jnp.float32) ** shard_levels(seeds[18], (FACE_BASIS, FAULTS), ((1, 512),), -0.2, 0.2), -3.0, -1.0),
    }


PRECISE = lax.Precision.HIGHEST
TIME_STEP = 0.1
GAUSS_NODES = (0.5 - 0.5 * math.sqrt(0.6), 0.5, 0.5 + 0.5 * math.sqrt(0.6))
GAUSS_WEIGHTS = (5.0 / 18.0, 8.0 / 18.0, 5.0 / 18.0)
PRESSURE_FLOOR = 0.25
SHEAR_FLOOR = 0.01
STATE_SCALE = 0.1
STATE_REFERENCE = 0.45
STATE_RATE = 0.2

def inverse_sinh(value):
    magnitude = jnp.abs(value)
    positive = jnp.log(magnitude + jnp.sqrt(1.0 + magnitude * magnitude))
    return jnp.where(value < 0.0, -positive, positive)

def jacobians(density, shear_modulus, lame_lambda):
    inverse = 1.0 / density
    stiffer = lame_lambda + 2.0 * shear_modulus
    empty_row = jnp.zeros_like(density)
    tables = ({(0, 6): -stiffer, (1, 6): -lame_lambda, (2, 6): -lame_lambda, (3, 7): -shear_modulus, (5, 8): -shear_modulus, (6, 0): -inverse, (7, 3): -inverse, (8, 5): -inverse}, {(0, 7): -lame_lambda, (1, 7): -stiffer, (2, 7): -lame_lambda, (3, 6): -shear_modulus, (4, 8): -shear_modulus, (6, 3): -inverse, (7, 1): -inverse, (8, 4): -inverse}, {(0, 8): -lame_lambda, (1, 8): -lame_lambda, (2, 8): -stiffer, (4, 7): -shear_modulus, (5, 6): -shear_modulus, (6, 5): -inverse, (7, 4): -inverse, (8, 2): -inverse})
    return jnp.stack([jnp.stack([jnp.stack([entries.get((target, source), empty_row) for source in range(9)]) for target in range(9)]) for entries in tables])

def element_setup(density, shear_modulus, lame_lambda, geometry):
    jacobian = jacobians(density, shear_modulus, lame_lambda)
    star_mats = jnp.einsum('dje,jqre->dqre', geometry, jacobian, precision=PRECISE)
    wave_speed = jnp.sqrt((lame_lambda + 2.0 * shear_modulus) / density)
    return (jacobian, star_mats, wave_speed)

def derivatives(modal, star_mats, stiffness):
    series = [modal]
    current = modal
    for degree in range(DERIVS - 1):
        mixed_terms = jnp.einsum('dqre,rbe->dqbe', star_mats, current, precision=PRECISE)
        current = jnp.einsum('dcb,dqbe->qce', stiffness, mixed_terms, precision=PRECISE)
        series.append(current)
    return series

def integrate(series, start_time, span_time):
    summed = 0.0
    for degree, series_term in enumerate(series):
        weight = ((start_time + span_time) ** (degree + 1) - start_time ** (degree + 1)) / math.factorial(degree + 1)
        summed = summed + weight * series_term
    return summed

def evaluate(series, moment):
    summed = 0.0
    for degree, series_term in enumerate(series):
        summed = summed + moment ** degree / math.factorial(degree) * series_term
    return summed

def volume(integral, star_mats, stiffness):
    mixed_terms = jnp.einsum('dqre,rbe->dqbe', star_mats, integral, precision=PRECISE)
    return jnp.einsum('dbc,dqbe->qce', stiffness, mixed_terms, precision=PRECISE)

def face_traces(integral, face_projection):
    traces = jnp.einsum('fcb,qbe->qcfe', face_projection, integral, precision=PRECISE)
    return traces.reshape(traces.shape[0], traces.shape[1], -1)

def lookup(own_flat, arrived, neighbour):
    trace_bank = jnp.concatenate([own_flat, arrived.reshape(own_flat.shape[0], own_flat.shape[1], -1), jnp.zeros((own_flat.shape[0], own_flat.shape[1], 2), own_flat.dtype)], axis=2)
    picked = jnp.take(trace_bank, neighbour.reshape(-1), axis=2)
    return picked.reshape(own_flat.shape[0], own_flat.shape[1], 4, -1)

def face_update(own_traces, neighbour_traces, normals, jacobian, wave_speed, lift_matrices, regular):
    normal_jacobian = jnp.einsum('fje,jqre->fqre', normals, jacobian, precision=PRECISE)
    damping = 0.5 * wave_speed[None, :] * lax.optimization_barrier(jnp.sum(jnp.abs(normals), axis=1))
    face_flux = 0.5 * jnp.einsum('fqre,rcfe->qcfe', normal_jacobian, own_traces + neighbour_traces, precision=PRECISE)
    face_flux = face_flux + damping[None, None] * (own_traces - neighbour_traces)
    face_flux = face_flux * regular[None, None]
    return jnp.einsum('fbc,qcfe->qbe', lift_matrices, face_flux, precision=PRECISE)

def fault_traces(series, positions, face_projection, elem_count):
    elements = positions % elem_count
    faces = positions // elem_count
    picked = [jnp.take(series_term, elements, axis=2) for series_term in series]
    projector = jnp.take(face_projection, faces, axis=0)
    results = []
    for node in GAUSS_NODES:
        at_time = evaluate(picked, node * TIME_STEP)
        results.append(jnp.einsum('jcb,qbj->qcj', projector, at_time, precision=PRECISE))
    return jnp.stack(results)

def fault_apply(imposed, positions, normals, jacobian, lift_matrices, elem_count):
    elements = positions % elem_count
    faces = positions // elem_count
    flat_normals = jnp.transpose(normals, (1, 0, 2)).reshape(3, -1)
    picked_normals = jnp.take(flat_normals, positions, axis=1)
    picked_jacobian = jnp.take(jacobian, elements, axis=3)
    normal_jacobian = jnp.einsum('jf,jqrf->qrf', picked_normals, picked_jacobian, precision=PRECISE)
    face_flux = jnp.einsum('qrf,rcf->qcf', normal_jacobian, imposed, precision=PRECISE)
    lifter = jnp.take(lift_matrices, faces, axis=0)
    lifted = jnp.einsum('fbc,qcf->qbf', lifter, face_flux, precision=PRECISE)
    return jnp.zeros((lifted.shape[0], lifted.shape[1], elem_count), lifted.dtype).at[:, :, elements].add(lifted)

def impedances(density, shear_modulus, lame_lambda, fault_plus, elem_count):
    elements = fault_plus % elem_count
    plus_density = jnp.take(density, elements)
    plus_modulus = jnp.take(shear_modulus, elements)
    plus_lambda = jnp.take(lame_lambda, elements)
    impedance_p = plus_density * jnp.sqrt((plus_lambda + 2.0 * plus_modulus) / plus_density)
    impedance_s = plus_density * jnp.sqrt(plus_modulus / plus_density)
    return (impedance_p, impedance_s)

def friction(plus, minus, impedance_p, impedance_s, direct_effect, shear_stress, normal_stress, slip_rate, fault_state):
    plus_total = 0.0
    minus_total = 0.0
    for node_index in range(len(GAUSS_NODES)):
        plus_now = plus[node_index]
        minus_now = minus[node_index]
        normal = 0.5 * (plus_now[0] + minus_now[0]) + 0.5 * impedance_p * (plus_now[6] - minus_now[6])
        shear_one = 0.5 * (plus_now[3] + minus_now[3]) + 0.5 * impedance_s * (plus_now[7] - minus_now[7]) + shear_stress[0]
        shear_two = 0.5 * (plus_now[5] + minus_now[5]) + 0.5 * impedance_s * (plus_now[8] - minus_now[8]) + shear_stress[1]
        pressure = jnp.maximum(-(normal_stress + normal), PRESSURE_FLOOR)
        locked = jnp.sqrt(jnp.maximum(shear_one * shear_one + shear_two * shear_two, SHEAR_FLOOR))
        damping = 0.5 * impedance_s
        factor = 0.5 * jnp.exp(fault_state / direct_effect)
        strength = pressure * direct_effect

        def newton(step_index, current):
            scaled = factor * current
            misfit = locked - damping * current - strength * inverse_sinh(scaled)
            newton_slope = -damping - strength * factor / jnp.sqrt(1.0 + scaled * scaled)
            return current - misfit / newton_slope
        slip_rate = lax.fori_loop(0, ITERS, newton, slip_rate)
        keep_ratio = (locked - damping * slip_rate) / locked
        traction_one = shear_one * keep_ratio
        traction_two = shear_two * keep_ratio
        weight = TIME_STEP * GAUSS_WEIGHTS[node_index]
        fault_state = fault_state + weight * STATE_RATE * (jnp.exp((STATE_REFERENCE - fault_state) / STATE_SCALE) - slip_rate)
        plus_rows = jnp.stack([normal, plus_now[1], plus_now[2], traction_one, plus_now[4], traction_two, plus_now[6] + (normal - plus_now[0]) / impedance_p, plus_now[7] + (traction_one - plus_now[3]) / impedance_s, plus_now[8] + (traction_two - plus_now[5]) / impedance_s])
        minus_rows = jnp.stack([normal, minus_now[1], minus_now[2], traction_one, minus_now[4], traction_two, minus_now[6] - (normal - minus_now[0]) / impedance_p, minus_now[7] - (traction_one - minus_now[3]) / impedance_s, minus_now[8] - (traction_two - minus_now[5]) / impedance_s])
        plus_total = plus_total + weight * plus_rows
        minus_total = minus_total + weight * minus_rows
    return (plus_total, minus_total, slip_rate, fault_state)

def per_device(array, width):
    shaped = array.reshape(array.shape[:-1] + (N_PARTS, width))
    return jnp.moveaxis(shaped, -2, 0)

def join_devices(array):
    moved = jnp.moveaxis(array, 0, -2)
    return moved.reshape(moved.shape[:-2] + (-1,))

def roll_traces(outgoing):
    pieces = []
    for direction, offset in enumerate((1, -1, STRIDE, -STRIDE)):
        pieces.append(jnp.roll(outgoing[:, :, :, direction], offset, axis=0))
    return jnp.stack(pieces, axis=3)

def reference(modal_state, density, shear_modulus, lame_lambda, geometry, normals, stiffness, face_projection, lift_matrices, cluster, neighbour, send_list, fault_plus, fault_minus, direct_effect, fault_state, slip_rate, shear_stress, normal_stress):
    device_block = (per_device(modal_state, E_DEV), per_device(density, E_DEV), per_device(shear_modulus, E_DEV), per_device(lame_lambda, E_DEV), per_device(geometry, E_DEV), per_device(normals, E_DEV), per_device(cluster, E_DEV), per_device(neighbour, E_DEV), per_device(send_list, SLOTS), per_device(fault_plus, F_DEV), per_device(fault_minus, F_DEV))

    def section_one(block_now):
        modal, dens, modulus, lamb, geom, norms, groups, links, outgoing_index, plus_pos, minus_pos = block_now
        jacobian, star_mats, wave_speed = element_setup(dens, modulus, lamb, geom)
        series = derivatives(modal, star_mats, stiffness)
        first_int = integrate(series, 0.0, TIME_STEP)
        second = integrate(series, TIME_STEP, TIME_STEP)
        own_flat = face_traces(first_int, face_projection)
        outgoing = jnp.take(own_flat, outgoing_index, axis=2)
        plus_traces = fault_traces(series, plus_pos, face_projection, E_DEV)
        minus_traces = fault_traces(series, minus_pos, face_projection, E_DEV)
        impedance_p, impedance_s = impedances(dens, modulus, lamb, plus_pos, E_DEV)
        return (first_int, second, outgoing, plus_traces, minus_traces, impedance_p, impedance_s)
    first_int, second, outgoing, plus_traces, minus_traces, impedance_p, impedance_s = lax.map(section_one, device_block)
    arrived_one = roll_traces(outgoing)
    wide_p = impedance_p[:, None, :]
    wide_s = impedance_s[:, None, :]
    effects = per_device(direct_effect, F_DEV)
    shears = jnp.moveaxis(per_device(shear_stress, F_DEV), 0, 1)
    normals_init = per_device(normal_stress, F_DEV)
    slips = per_device(slip_rate, F_DEV)
    states = per_device(fault_state, F_DEV)
    minus_arrived = jnp.roll(minus_traces, -STRIDE, axis=0)
    plus_one, minus_one, slips, states = friction(jnp.moveaxis(plus_traces, 0, 2), jnp.moveaxis(minus_arrived, 0, 2), wide_p, wide_s, effects, shears, normals_init, slips, states)
    plus_one = jnp.moveaxis(plus_one, 1, 0)
    minus_one = jnp.roll(jnp.moveaxis(minus_one, 1, 0), STRIDE, axis=0)

    def section_two(inputs):
        block_now, first_now, second_now, arrived_now, plus_now, minus_now = inputs
        modal, dens, modulus, lamb, geom, norms, groups, links, outgoing_index, plus_pos, minus_pos = block_now
        jacobian, star_mats, wave_speed = element_setup(dens, modulus, lamb, geom)
        regular = (links <= 4 * E_DEV + 4 * SLOTS).astype(jnp.float32)
        own_flat = face_traces(first_now, face_projection)
        neighbour_traces = lookup(own_flat, arrived_now, links)
        surface = face_update(own_flat.reshape(own_flat.shape[0], own_flat.shape[1], 4, -1), neighbour_traces, norms, jacobian, wave_speed, lift_matrices, regular)
        partial_state = modal + volume(first_now, star_mats, stiffness) - surface
        partial_state = partial_state - fault_apply(plus_now, plus_pos, norms, jacobian, lift_matrices, E_DEV)
        partial_state = partial_state - fault_apply(minus_now, minus_pos, norms, jacobian, lift_matrices, E_DEV)
        fast_mask = (groups == 0)[None, None]
        updated = jnp.where(fast_mask, partial_state, modal)
        later_series = derivatives(updated, star_mats, stiffness)
        second_int = jnp.where(fast_mask, integrate(later_series, 0.0, TIME_STEP), second_now)
        own_second = face_traces(second_int, face_projection)
        outgoing_two = jnp.take(own_second, outgoing_index, axis=2)
        plus_two = fault_traces(later_series, plus_pos, face_projection, E_DEV)
        minus_two = fault_traces(later_series, minus_pos, face_projection, E_DEV)
        return (partial_state, second_int, outgoing_two, plus_two, minus_two)
    partial_state, second_int, outgoing_two, plus_traces, minus_traces = lax.map(section_two, (device_block, first_int, second, arrived_one, plus_one, minus_one))
    arrived_two = roll_traces(outgoing_two)
    minus_arrived = jnp.roll(minus_traces, -STRIDE, axis=0)
    plus_two, minus_two, slips, states = friction(jnp.moveaxis(plus_traces, 0, 2), jnp.moveaxis(minus_arrived, 0, 2), wide_p, wide_s, effects, shears, normals_init, slips, states)
    plus_two = jnp.moveaxis(plus_two, 1, 0)
    minus_two = jnp.roll(jnp.moveaxis(minus_two, 1, 0), STRIDE, axis=0)

    def section_three(inputs):
        block_now, partial_now, second_now, arrived_now, plus_now, minus_now = inputs
        modal, dens, modulus, lamb, geom, norms, groups, links, outgoing_index, plus_pos, minus_pos = block_now
        jacobian, star_mats, wave_speed = element_setup(dens, modulus, lamb, geom)
        regular = (links <= 4 * E_DEV + 4 * SLOTS).astype(jnp.float32)
        own_flat = face_traces(second_now, face_projection)
        neighbour_traces = lookup(own_flat, arrived_now, links)
        surface = face_update(own_flat.reshape(own_flat.shape[0], own_flat.shape[1], 4, -1), neighbour_traces, norms, jacobian, wave_speed, lift_matrices, regular)
        final_state = partial_now + volume(second_now, star_mats, stiffness) - surface
        final_state = final_state - fault_apply(plus_now, plus_pos, norms, jacobian, lift_matrices, E_DEV)
        final_state = final_state - fault_apply(minus_now, minus_pos, norms, jacobian, lift_matrices, E_DEV)
        return final_state
    final_state = lax.map(section_three, (device_block, partial_state, second_int, arrived_two, plus_two, minus_two))
    return (join_devices(final_state), join_devices(slips), join_devices(states))
```

```python
import functools
import math

import jax
import jax.numpy as jnp
from jax import lax
from jax.experimental import pallas as pl
from jax.experimental.pallas import tpu as pltpu
from jax.sharding import PartitionSpec as P

DERIVS = 4
ITERS = 10
STRIDE = 8

TIME_STEP = 0.1
GAUSS_NODES = (0.5 - 0.5 * math.sqrt(0.6), 0.5, 0.5 + 0.5 * math.sqrt(0.6))
GAUSS_WEIGHTS = (5.0 / 18.0, 8.0 / 18.0, 5.0 / 18.0)
PRESSURE_FLOOR = 0.25
SHEAR_FLOOR = 0.01
STATE_SCALE = 0.1
STATE_REFERENCE = 0.45
STATE_RATE = 0.2

F32 = jnp.float32
BF16 = jnp.bfloat16
L = 128
BASIS = 35
BROWS = 40
POINTS = 21
PROWS = 24
QUANTITIES = 9
FACES = 4
TROWS = 224
GROUP = 48
CROWS = 80
PAIRS = ((0, 6, 0), (3, 7, 1), (5, 8, 1))
SIGMA = ((0, 3, 5), (3, 1, 4), (5, 4, 2))


LOAD_ORDER = (0, 6, 4, 1, 2, 3, 7, 12, 13, 17, 18, 5, 8, 9, 10, 11, 14, 15, 16)


def split(value):
    high = value.astype(BF16)
    low = (value - high.astype(F32)).astype(BF16)
    return high, low


def pick(rows, selector):
    count = rows.shape[0]
    stacked = jnp.concatenate(split(rows), axis=0)
    result = jnp.dot(stacked, selector, preferred_element_type=F32)
    return result[:count] + result[count:]


def pick_exact(rows, selector):
    high = rows.astype(BF16)
    rest = rows - high.astype(F32)
    middle = rest.astype(BF16)
    low = (rest - middle.astype(F32)).astype(BF16)
    result = jnp.dot(high, selector, preferred_element_type=F32)
    result = result + jnp.dot(middle, selector, preferred_element_type=F32)
    return result + jnp.dot(low, selector, preferred_element_type=F32)


def ones_where(mask):
    return jnp.where(mask, 1.0, 0.0).astype(BF16)


def inverse_sinh(value):
    magnitude = jnp.abs(value)
    positive = jnp.log(magnitude + jnp.sqrt(1.0 + magnitude * magnitude))
    return jnp.where(value < 0.0, -positive, positive)


def strain_like(coefs, velocity):
    c0, c1, c2 = coefs
    u, v, w = velocity
    return [c0 * u, c1 * v, c2 * w, c1 * u + c0 * v, c2 * v + c1 * w, c2 * u + c0 * w]


def stress_along(coefs, stress):
    return [
        coefs[0] * stress[row[0]] + coefs[1] * stress[row[1]] + coefs[2] * stress[row[2]]
        for row in SIGMA
    ]


def materials_applied(lam, mu, inverse, strain, force):
    spread = lam * (strain[0] + strain[1] + strain[2])
    twice = 2.0 * mu
    return (
        [-(spread + twice * strain[i]) for i in range(3)]
        + [-(mu * strain[i]) for i in range(3, 6)]
        + [-(inverse * force[i]) for i in range(3)]
    )


def kernel(
    size,
    *refs,
):
    inputs = refs[:19]
    (
        out_ref,
        out_slip_ref,
        out_state_ref,
        pads,
        tall,
        w_dv,
        w_vol,
        w_trace,
        w_lift,
        series,
        second,
        base,
        rhs,
        rhs_trace,
        rhs_time,
        traces,
        tight,
        chars,
        sums,
        sel_fault,
        sel_face,
        sel_own,
        sel_arrived,
        sel_send,
        density_far,
        modulus_far,
        lambda_far,
        plus_far,
        direct_far,
        state_far,
        slip_far,
        normal_far,
        char_send,
        char_recv,
        trace_send,
        trace_recv,
        first_send_sem,
        first_recv_sem,
        char_send_sem,
        char_recv_sem,
        trace_send_sem,
        trace_recv_sem,
        input_sem,
    ) = refs[19:-19]
    held = refs[-19:]
    (
        modal_ref,
        density_ref,
        modulus_ref,
        lambda_ref,
        geometry_ref,
        normals_ref,
        stiffness_ref,
        projection_ref,
        lift_ref,
        cluster_ref,
        neighbour_ref,
        send_list_ref,
        plus_ref,
        minus_ref,
        direct_ref,
        state_ref,
        slip_ref,
        shear_ref,
        normal_ref,
    ) = held
    me = lax.axis_index("parts")
    up = lax.rem(me + 1, size)
    down = lax.rem(me + size - 1, size)
    ahead = lax.rem(me + STRIDE, size)
    behind = lax.rem(me + size - STRIDE, size)

    def remote(source, target, send_sem, recv_sem, device):
        return pltpu.make_async_remote_copy(
            src_ref=source,
            dst_ref=target,
            send_sem=send_sem,
            recv_sem=recv_sem,
            device_id=(device,),
            device_id_type=pl.DeviceIdType.MESH,
        )

    barrier = pltpu.get_barrier_semaphore()
    for partner in (up, down, ahead, behind):
        pl.semaphore_signal(
            barrier, inc=1, device_id=(partner,), device_id_type=pl.DeviceIdType.MESH
        )

    loads = [
        pltpu.make_async_copy(inputs[i], held[i], input_sem.at[i]) for i in range(len(inputs))
    ]
    for i in LOAD_ORDER:
        loads[i].start()

    def wait_inputs(*numbers):
        for i in numbers:
            loads[i].wait()

    def impedances(rho, mu, lam, positions):
        zp = rho * jnp.sqrt((lam + 2.0 * mu) / rho)
        zs = rho * jnp.sqrt(mu / rho)
        row = lax.broadcasted_iota(jnp.int32, (16, L), 0)
        rows = jnp.where(row == 0, zp, jnp.where(row == 1, zs, 0.0))
        elements = lax.rem(positions, L)
        hit = lax.broadcasted_iota(jnp.int32, (L, L), 0) == elements
        picked = pick_exact(rows, ones_where(hit))
        return [picked[i : i + 1] for i in range(2)]

    wait_inputs(0, 1, 2, 3, 4, 6, 7, 12, 13)
    rho = density_ref[...]
    mu = modulus_ref[...]
    lam = lambda_ref[...]
    inverse = 1.0 / rho
    wave_speed = jnp.sqrt((lam + 2.0 * mu) / rho)

    plus_at = plus_ref[...]
    minus_at = minus_ref[...]
    face_rows = lax.broadcasted_iota(jnp.int32, (FACES * L, L), 0)
    sel_fault[:, 0:L] = ones_where(face_rows == plus_at)
    sel_fault[:, L : 2 * L] = ones_where(face_rows == minus_at)
    z_plus = impedances(rho, mu, lam, plus_at)

    pads[...] = jnp.zeros(pads.shape, F32)
    tall[...] = jnp.zeros(tall.shape, F32)
    for d in range(3):
        pads[d * BROWS : d * BROWS + BASIS, 0:BASIS] = stiffness_ref[d]
    for f in range(FACES):
        tall[f * PROWS : f * PROWS + POINTS, 0:BASIS] = projection_ref[:, f, :]

    def side_by_side(matrix):
        high, low = split(matrix)
        high = high.astype(F32)
        low = low.astype(F32)
        top = jnp.concatenate([high, high], axis=1)
        bottom = jnp.concatenate([low, jnp.zeros_like(low)], axis=1)
        return jnp.concatenate([top, bottom], axis=0).astype(BF16)

    stiff_rows = pads[...]
    flat = stiff_rows[0:BROWS]
    for d in range(1, 3):
        flat = flat + pltpu.roll(stiff_rows[d * BROWS : (d + 1) * BROWS], d * BROWS, 1)
    w_dv[...] = side_by_side(flat)

    high, low = split(tall[...])
    high = high.astype(F32)
    low = pltpu.roll(low.astype(F32), 96, 1)
    lane = lax.broadcasted_iota(jnp.int32, (FACES * PROWS, L), 1)
    left = high + pltpu.roll(high, 48, 1) + jnp.where(lane >= 96, low, 0.0)
    right = jnp.where(lane < 32, low, 0.0)
    w_trace[...] = jnp.concatenate([left, right], axis=1).astype(BF16)

    for q in range(QUANTITIES):
        series[0, q, BASIS - 3 : BROWS, :] = jnp.zeros((BROWS - BASIS + 3, L), F32)
        series[0, q, 0:BASIS, :] = modal_ref[q]

    geometry = [[geometry_ref[d, j : j + 1, :] for j in range(3)] for d in range(3)]

    def fill(columns):
        for q, blocks in enumerate(columns):
            used = sum(block.shape[0] for block in blocks)
            whole = jnp.concatenate(blocks + [jnp.zeros((L - used, L), F32)], axis=0)
            high, low = split(whole)
            rhs[0:L, q * L : (q + 1) * L] = high
            rhs[L : 2 * L, q * L : (q + 1) * L] = low

    def multiplied(weights):
        result = jnp.dot(weights[...], rhs[...], preferred_element_type=F32)
        result = result[0:BROWS] + result[BROWS : 2 * BROWS]
        return [result[:, q * L : (q + 1) * L] for q in range(QUANTITIES)]

    def stiff_apply(weights, field):
        strains = [strain_like(geometry[d], field[6:9]) for d in range(3)]
        forces = [stress_along(geometry[d], field[0:6]) for d in range(3)]
        fill(
            [[strains[d][i] for d in range(3)] for i in range(6)]
            + [[forces[d][i] for d in range(3)] for i in range(3)]
        )
        result = multiplied(weights)
        return materials_applied(lam, mu, inverse, result[0:6], result[6:9])

    def derive():
        for k in range(DERIVS - 1):
            field = [series[k, q] for q in range(QUANTITIES)]
            for q, value in enumerate(stiff_apply(w_dv, field)):
                series[k + 1, q] = value

    def integral(q, start, span):
        total = 0.0
        for k in range(DERIVS):
            weight = ((start + span) ** (k + 1) - start ** (k + 1)) / math.factorial(k + 1)
            total = total + weight * series[k, q]
        return total

    def put_trace_column(target, column, value):
        whole = jnp.concatenate([value, jnp.zeros((48 - BROWS, L), F32)], axis=0)
        high, low = split(whole)
        place = slice(column * L, (column + 1) * L)
        target[0:48, place] = high
        target[48:96, place] = low
        target[96:144, place] = high

    traces[TROWS - 8 : TROWS, :] = jnp.zeros((8, FACES * L), F32)
    sums[...] = jnp.zeros(sums.shape, F32)
    for side in range(2):
        for m in range(3):
            for number in range(2):
                char_send[number, side, m, 56:64, :] = jnp.zeros((8, L), F32)

    derive()

    def pick_chars(m):
        moment = GAUSS_NODES[m] * TIME_STEP
        for n, (stress, velocity, which) in enumerate(PAIRS):
            for i, q in enumerate((stress, velocity)):
                value = series[2, q] + (moment / 3.0) * series[3, q]
                value = series[1, q] + (moment / 2.0) * value
                value = series[0, q] + moment * value
                put_trace_column(rhs_time, 2 * n + i, value)
        result = jnp.dot(w_trace[:, 0:144], rhs_time[...], preferred_element_type=F32)
        for k in range(6):
            for f in range(FACES):
                chars[k * PROWS : (k + 1) * PROWS, f * L : (f + 1) * L] = result[
                    f * PROWS : (f + 1) * PROWS, k * L : (k + 1) * L
                ]
        return pick(chars[...], sel_fault[...])

    def send_chars(number, side, m, picked, extra):
        lanes = slice(side * L, (side + 1) * L)
        for n, (stress, velocity, which) in enumerate(PAIRS):
            upper = picked[2 * n * PROWS : 2 * n * PROWS + POINTS, lanes]
            lower = picked[(2 * n + 1) * PROWS : (2 * n + 1) * PROWS + POINTS, lanes]
            if side == 0:
                value = upper + z_plus[which] * lower + extra[n]
            else:
                value = upper - z_far[which] * lower
            char_send[number, side, m, n * POINTS : (n + 1) * POINTS, :] = value
        copy = remote(
            char_send.at[number, side, m],
            char_recv.at[number, 1 - side, m],
            char_send_sem.at[number, side, m],
            char_recv_sem.at[number, 1 - side, m],
            (ahead, behind)[side],
        )
        copy.start()
        return copy

    slots = send_list_ref.shape[1]
    lane_groups = lax.broadcasted_iota(jnp.int32, (GROUP, L), 1) // slots

    def pack_traces(number, integrals):
        for q in range(QUANTITIES):
            put_trace_column(rhs_trace, q, integrals[q])
        result = jnp.dot(w_trace[:, 0:144], rhs_trace[...], preferred_element_type=F32)
        for q in range(QUANTITIES):
            for f in range(FACES):
                traces[q * PROWS : (q + 1) * PROWS, f * L : (f + 1) * L] = result[
                    f * PROWS : (f + 1) * PROWS, q * L : (q + 1) * L
                ]
        outgoing = pick(traces[...], sel_send[...])
        for q in range(QUANTITIES):
            tight[q * POINTS : q * POINTS + PROWS, :] = outgoing[q * PROWS : (q + 1) * PROWS]
        copies = []
        for r, device in enumerate((up, down, ahead, behind)):
            packed = jnp.zeros((GROUP, L), F32)
            for g in range(4):
                rows = tight[g * GROUP : (g + 1) * GROUP, :]
                shift = ((g - r) * slots) % L
                rows = pltpu.roll(rows, shift, 1) if shift else rows
                packed = jnp.where(lane_groups == g, rows, packed)
            trace_send[number, r] = packed
            copy = remote(
                trace_send.at[number, r],
                trace_recv.at[number, r],
                trace_send_sem.at[number, r],
                trace_recv_sem.at[number, r],
                device,
            )
            copies.append(copy)
        return copies

    def arrived_traces(number):
        for g in range(4):
            rows_g = jnp.zeros((GROUP, L), F32)
            for r in range(4):
                rows = trace_recv[number, r]
                shift = ((r - g) * slots) % L
                rows = pltpu.roll(rows, shift, 1) if shift else rows
                rows_g = jnp.where(lane_groups == r, rows, rows_g)
            tight[g * GROUP : (g + 1) * GROUP, :] = rows_g
        blocks = [tight[q * POINTS : q * POINTS + PROWS, :] for q in range(QUANTITIES)]
        return jnp.concatenate(blocks + [jnp.zeros((8, L), F32)], axis=0)

    def friction(number, copies, slip, state, direct):
        totals = [0.0, 0.0, 0.0]
        for m in range(3):
            mean = []
            for side in range(2):
                copies[side][m].wait_recv()
            for n in range(3):
                rows = slice(n * POINTS, (n + 1) * POINTS)
                halves = [
                    0.5 * (char_send[number, side, m, rows, :] + char_recv[number, side, m, rows, :])
                    for side in range(2)
                ]
                mean.append(jnp.concatenate(halves, axis=1))
            loaded, shear_one, shear_two = mean
            pressure = jnp.maximum(-loaded, PRESSURE_FLOOR)
            locked = jnp.sqrt(
                jnp.maximum(shear_one * shear_one + shear_two * shear_two, SHEAR_FLOOR)
            )
            factor = 0.5 * jnp.exp(state / direct)
            strength = pressure * direct
            slope_scale = strength * factor

            def newton(step, current):
                scaled = factor * current
                misfit = locked - eta * current - strength * inverse_sinh(scaled)
                slope = -eta - slope_scale / jnp.sqrt(1.0 + scaled * scaled)
                return current - misfit / slope

            slip = lax.fori_loop(0, ITERS, newton, slip, unroll=True)
            keep = (locked - eta * slip) / locked
            weight = TIME_STEP * GAUSS_WEIGHTS[m]
            state = state + weight * STATE_RATE * (
                jnp.exp((STATE_REFERENCE - state) / STATE_SCALE) - slip
            )
            totals[0] = totals[0] + weight * (loaded - normal)
            totals[1] = totals[1] + weight * (shear_one * keep)
            totals[2] = totals[2] + weight * (shear_two * keep)
        return totals, slip, state

    def surface(number, nearby, copies, totals):
        for n in range(3):
            sums[n * PROWS : n * PROWS + POINTS, :] = totals[n]
        imposed = pick(sums[...], sel_face[...])
        for copy in copies:
            copy.wait_recv()
        others = nearby + pick(arrived_traces(number), sel_arrived[...])
        blocks = [[] for q in range(QUANTITIES)]
        for f in range(FACES):
            place = slice(f * L, (f + 1) * L)
            mine = [traces[q * PROWS : (q + 1) * PROWS, place] for q in range(QUANTITIES)]
            other = [others[q * PROWS : (q + 1) * PROWS, place] for q in range(QUANTITIES)]
            given = [imposed[n * PROWS : (n + 1) * PROWS, place] for n in range(3)]
            state = [given[0], mine[1], mine[2], given[1], mine[4], given[2], None, None, None]
            for n, (stress, velocity, which) in enumerate(PAIRS):
                state[velocity] = (
                    mine[velocity] + (given[n] - mine[stress]) * z_inverse[which][f]
                )
            mixed = [
                jnp.where(regular[f], 0.5 * (mine[q] + other[q]), state[q])
                for q in range(QUANTITIES)
            ]
            damped = jnp.where(regular[f], damping[f], 0.0)
            flux = materials_applied(
                lam, mu, inverse, strain_like(normals[f], mixed[6:9]), stress_along(normals[f], mixed)
            )
            for q in range(QUANTITIES):
                blocks[q].append(flux[q] + damped * (mine[q] - other[q]))
        fill(blocks)
        return multiplied(w_lift)

    def start_traces(copies, sent, after=()):
        copies[0].start()
        copies[1].start()
        sent[0][2].wait_send()
        for copy in after:
            copy.start()
        copies[2].start()
        sent[1][2].wait_send()
        copies[3].start()

    def params(near, far):
        return jnp.concatenate([near, far], axis=1)

    wait_inputs(17, 18)
    extra = [2.0 * normal_ref[...], 2.0 * shear_ref[:, 0, :], 2.0 * shear_ref[:, 1, :]]
    picked = [pick_chars(0)]
    pl.semaphore_wait(barrier, 4)
    first = [
        remote(inputs[i], far, first_send_sem.at[n], first_recv_sem.at[n], ahead)
        for n, (i, far) in enumerate(
            (
                (1, density_far),
                (2, modulus_far),
                (3, lambda_far),
                (12, plus_far),
                (15, state_far),
                (14, direct_far),
                (16, slip_far),
                (18, normal_far),
            )
        )
    ]
    for copy in first[0:4]:
        copy.start()

    sent = [[send_chars(0, 0, 0, picked[0], extra)]]
    for m in range(1, 3):
        picked.append(pick_chars(m))
        sent[0].append(send_chars(0, 0, m, picked[m], extra))
    for copy in first[0:4]:
        copy.wait_recv()
    z_far = impedances(density_far[...], modulus_far[...], lambda_far[...], plus_far[...])
    sent.append([send_chars(0, 1, m, picked[m], extra) for m in range(3)])

    wait_inputs(5, 8, 9, 10, 11)
    w_vol[...] = side_by_side(jnp.transpose(stiff_rows)[0:BROWS])
    pads[...] = jnp.zeros(pads.shape, F32)
    for f in range(FACES):
        pads[f * PROWS : f * PROWS + POINTS, 0:BASIS] = lift_ref[:, f, :]
    flat = jnp.transpose(pads[...])[0:BROWS]
    w_lift[...] = side_by_side(flat)
    normals = [[normals_ref[j, f : f + 1, :] for j in range(3)] for f in range(FACES)]
    pos_rows = jnp.concatenate(
        [
            jnp.transpose(jnp.broadcast_to(plus_at.astype(F32), (L, L))),
            jnp.transpose(jnp.broadcast_to(minus_at.astype(F32), (L, L))),
        ],
        axis=0,
    )
    lane_id = lax.broadcasted_iota(jnp.int32, (2 * L, L), 1).astype(F32)
    for f in range(FACES):
        place = slice(f * L, (f + 1) * L)
        sel_face[:, place] = ones_where(pos_rows == lane_id + float(f * L))
        here = neighbour_ref[f : f + 1, :]
        sel_own[:, place] = ones_where(face_rows == here)
        sel_arrived[:, place] = ones_where(face_rows[0:L] == here - FACES * L)
    spread_slots = jnp.where(
        lax.rem(lax.broadcasted_iota(jnp.int32, (slots, L), 1), slots)
        == lax.broadcasted_iota(jnp.int32, (slots, L), 0),
        1.0,
        0.0,
    )
    wanted = jnp.dot(
        send_list_ref[...].astype(F32),
        spread_slots,
        precision=lax.Precision.HIGHEST,
        preferred_element_type=F32,
    )
    lane_group = lax.broadcasted_iota(jnp.int32, (1, L), 1) // slots
    sent_row = jnp.zeros((1, L), F32)
    for r in range(4):
        sent_row = jnp.where(lane_group == r, wanted[r : r + 1], sent_row)
    sel_send[...] = ones_where(face_rows == (sent_row + 0.5).astype(jnp.int32))

    integrals = [integral(q, 0.0, TIME_STEP) for q in range(QUANTITIES)]
    trace_copies = pack_traces(0, integrals)
    start_traces(trace_copies, sent, first[4:])

    z_fault = [jnp.concatenate([z_plus[i], z_far[i]], axis=1) for i in range(2)]
    row_side = lax.broadcasted_iota(jnp.int32, (16, 2 * L), 0)
    lane_side = lax.broadcasted_iota(jnp.int32, (1, 2 * L), 1)
    sign = jnp.where(lane_side < L, 1.0, -1.0)
    z_signed = jnp.where(
        row_side == 0, sign * z_fault[0], jnp.where(row_side == 1, sign * z_fault[1], 0.0)
    )
    z_face = pick_exact(z_signed, sel_face[...])
    z_inverse_rows = 1.0 / jnp.where(z_face == 0.0, 1.0, z_face)
    z_inverse = [
        [z_inverse_rows[i : i + 1, f * L : (f + 1) * L] for f in range(FACES)] for i in range(2)
    ]
    eta = 0.5 * z_fault[1]
    fast = cluster_ref[...] == 0
    regular = [neighbour_ref[f : f + 1, :] <= FACES * L + 4 * slots for f in range(FACES)]
    damping = [
        0.5
        * wave_speed
        * (jnp.abs(normals[f][0]) + jnp.abs(normals[f][1]) + jnp.abs(normals[f][2]))
        for f in range(FACES)
    ]
    for q in range(QUANTITIES):
        second[q] = integral(q, TIME_STEP, TIME_STEP)
    for q, value in enumerate(stiff_apply(w_vol, integrals)):
        base[q] = series[0, q] + value
    nearby = pick(traces[...], sel_own[...])
    wait_inputs(14, 15, 16)
    for copy in first[4:]:
        copy.wait_recv()
    direct = params(direct_ref[...], direct_far[...])
    normal = params(normal_ref[...], normal_far[...])
    slip = params(slip_ref[...], slip_far[...])
    state = params(state_ref[...], state_far[...])
    totals, slip, state = friction(0, sent, slip, state, direct)
    lifted = surface(0, nearby, trace_copies, totals)
    for q in range(QUANTITIES):
        partial = base[q] - lifted[q]
        base[q] = partial
        series[0, q] = jnp.where(fast, partial, series[0, q])
    started = first + sent[0][:2] + sent[1][:2] + trace_copies

    derive()
    sent = [[], []]
    for m in range(3):
        picked = pick_chars(m)
        for side in range(2):
            sent[side].append(send_chars(1, side, m, picked, extra))
    integrals = [
        jnp.where(fast, integral(q, 0.0, TIME_STEP), second[q]) for q in range(QUANTITIES)
    ]
    trace_copies = pack_traces(1, integrals)
    start_traces(trace_copies, sent)
    for q, value in enumerate(stiff_apply(w_vol, integrals)):
        base[q] = base[q] + value
    nearby = pick(traces[...], sel_own[...])
    totals, slip, state = friction(1, sent, slip, state, direct)
    out_slip_ref[...] = slip[:, 0:L]
    out_state_ref[...] = state[:, 0:L]
    lifted = surface(1, nearby, trace_copies, totals)
    for q in range(QUANTITIES):
        out_ref[q] = (base[q] - lifted[q])[0:BASIS]
    for copy in started + sent[0][:2] + sent[1][:2] + trace_copies:
        copy.wait_send()


def per_device(size, modal_state, density, shear_modulus, lame_lambda, geometry, normals, stiffness,
               face_projection, lift_matrices, cluster, neighbour, send_list, fault_plus, fault_minus,
               direct_effect, fault_state, slip_rate, shear_stress, normal_stress):
    row = (1, L)
    operands = (
        modal_state,
        density.reshape(row),
        shear_modulus.reshape(row),
        lame_lambda.reshape(row),
        geometry,
        jnp.transpose(normals, (1, 0, 2)),
        stiffness,
        jnp.transpose(face_projection, (1, 0, 2)),
        jnp.transpose(lift_matrices, (2, 0, 1)),
        cluster.reshape(row),
        neighbour,
        send_list,
        fault_plus.reshape(row),
        fault_minus.reshape(row),
        direct_effect,
        fault_state,
        slip_rate,
        jnp.transpose(shear_stress, (1, 0, 2)),
        normal_stress,
    )
    vmem = pl.BlockSpec(memory_space=pltpu.VMEM)
    points = pltpu.VMEM((POINTS, L), F32)
    return pl.pallas_call(
        functools.partial(kernel, size),
        out_shape=(
            pltpu.VMEM(modal_state.shape, F32),
            pltpu.VMEM(slip_rate.shape, F32),
            pltpu.VMEM(fault_state.shape, F32),
        ),
        in_specs=[pl.BlockSpec(memory_space=pltpu.HBM)] * len(operands),
        out_specs=(vmem, vmem, vmem),
        scratch_shapes=[
            pltpu.VMEM((L, L), F32),
            pltpu.VMEM((FACES * PROWS, L), F32),
            pltpu.VMEM((2 * BROWS, 2 * L), BF16),
            pltpu.VMEM((2 * BROWS, 2 * L), BF16),
            pltpu.VMEM((FACES * PROWS, 2 * L), BF16),
            pltpu.VMEM((2 * BROWS, 2 * L), BF16),
            pltpu.VMEM((DERIVS, QUANTITIES, BROWS, L), F32),
            pltpu.VMEM((QUANTITIES, BROWS, L), F32),
            pltpu.VMEM((QUANTITIES, BROWS, L), F32),
            pltpu.VMEM((2 * L, QUANTITIES * L), BF16),
            pltpu.VMEM((144, QUANTITIES * L), BF16),
            pltpu.VMEM((144, 6 * L), BF16),
            pltpu.VMEM((TROWS, FACES * L), F32),
            pltpu.VMEM((4 * GROUP, L), F32),
            pltpu.VMEM((6 * PROWS, FACES * L), F32),
            pltpu.VMEM((CROWS, 2 * L), F32),
            pltpu.VMEM((FACES * L, 2 * L), BF16),
            pltpu.VMEM((2 * L, FACES * L), BF16),
            pltpu.VMEM((FACES * L, FACES * L), BF16),
            pltpu.VMEM((L, FACES * L), BF16),
            pltpu.VMEM((FACES * L, L), BF16),
            pltpu.VMEM(row, F32),
            pltpu.VMEM(row, F32),
            pltpu.VMEM(row, F32),
            pltpu.VMEM(row, jnp.int32),
            points,
            points,
            points,
            points,
            pltpu.VMEM((2, 2, 3, 64, L), F32),
            pltpu.VMEM((2, 2, 3, 64, L), F32),
            pltpu.VMEM((2, 4, GROUP, L), F32),
            pltpu.VMEM((2, 4, GROUP, L), F32),
            pltpu.SemaphoreType.DMA((8,)),
            pltpu.SemaphoreType.DMA((8,)),
            pltpu.SemaphoreType.DMA((2, 2, 3)),
            pltpu.SemaphoreType.DMA((2, 2, 3)),
            pltpu.SemaphoreType.DMA((2, 4)),
            pltpu.SemaphoreType.DMA((2, 4)),
            pltpu.SemaphoreType.DMA((len(operands),)),
            *[pltpu.VMEM(x.shape, x.dtype) for x in operands],
        ],
        compiler_params=pltpu.CompilerParams(
            collective_id=0, has_side_effects=True, vmem_limit_bytes=58 * 2**20
        ),
    )(*operands)


def solution(mesh):
    along = P("parts")
    one = P(None, "parts")
    two = P(None, None, "parts")
    return jax.shard_map(
        functools.partial(per_device, mesh.shape["parts"]),
        mesh=mesh,
        in_specs=(two, along, along, along, two, two, P(), P(), P(), along, one, one, along, along,
                  one, one, one, two, one),
        out_specs=(two, one, one),
        check_vma=False,
    )
```
